256 devices in a mesh: worker: 32 (over z_lo, x, core), shard: 8 (over y, z_hi).
Axes of the slice: x: 4, y: 4, z: 8 (z_hi: 2, z_lo: 4; z = z_hi * 4 + z_lo), core: 2. Of those that a mesh axis runs over, the one named last changes fastest.
Arguments:
- local_w: bfloat16 [32, 2048, 4608], P('worker', 'shard'), may hold values from -36 to 36
- base_w: float32 [2048, 4608], P('shard'), may hold values from -6 to 6
- momentum: float32 [2048, 4608], P(('shard', 'worker')), may hold values from -3 to 3
Outputs:
- new_base: float32 [2048, 4608], P('shard')
- new_momentum: float32 [2048, 4608], P(('shard', 'worker'))
The draws below stay inside these ranges and needn't reach their ends.
All inputs are finite; a program needn't handle non-finite values.
Results may differ from the reference program's by a relative error of at most 0.028.
Values may be sent and summed in bfloat16 or wider, within the bound.
A program may use at most 64 MiB of HBM per device.

```python
import math
import jax
import jax.numpy as jnp
from jax import lax

D = 4608
BLOCK = 128
WORKERS = 32
FFW = 2048


def draw_local_w(key, part):
    key = jax.random.fold_in(key, 11)
    private_key, row_key, col_key = jax.random.split(key, 3)
    lowest_log = math.log(0.3)
    highest_log = math.log(3.0)
    row_scale = jnp.exp(jax.random.uniform(row_key, (WORKERS, FFW, 1), jnp.float32, lowest_log, highest_log))
    col_scale = jnp.exp(jax.random.uniform(col_key, (1, 1, D), jnp.float32, lowest_log, highest_log))
    private_part = jnp.clip(jax.random.normal(private_key, (WORKERS, FFW, D), jnp.float32), -4.0, 4.0)
    values = private_part * row_scale * col_scale
    return values.astype(jnp.bfloat16)


def shard_levels(own_key, dims, cuts, least, top_value):
    loudness, own = 1.0, jax.random.fold_in(own_key, 6)
    for position, blocks in cuts:
        steps = jnp.exp(jax.random.uniform(jax.random.fold_in(own, position), (blocks,), jnp.float32, least / len(cuts), top_value / len(cuts)))
        loudness = loudness * jnp.repeat(steps, dims[position] // blocks).reshape([-1 if axis == position else 1 for axis in range(len(dims))])
    return loudness


def centred(stream_key, shape, scale, bound, cuts=(), dtype=jnp.bfloat16):
    values = scale * jax.random.normal(stream_key, shape, jnp.float32)
    if cuts:
        values = values * shard_levels(stream_key, shape, cuts, -0.22, 0.18)
    return jnp.clip(values, -bound, bound).astype(dtype)


def setup_inputs(seed: int = 0) -> dict:
    seeds = jax.random.split(jax.random.key(seed), 4)
    local_w = draw_local_w(jax.random.fold_in(seeds[3], 71), 0)
    base_w = centred(seeds[1], (FFW, D), 1.0, 6.0, ((0, 8),), jnp.float32)
    momentum = centred(seeds[2], (FFW, D), 0.5, 3.0, ((0, 256),), jnp.float32)
    return dict(local_w=local_w, base_w=base_w, momentum=momentum)


epsilon = 1e-06
CODE_LIMIT = 448.0
CLIP_WIDTH = 2.0
NESTEROV_MU = 0.9
OUTER_RATE = 0.7

def rotate(values):
    leading = values.shape[:-1]
    columns = values.shape[-1]
    blocks = values.reshape(leading + (columns // BLOCK, BLOCK))
    stride_len = 1
    for bit_pos in range(BLOCK.bit_length() - 1):
        paired = blocks.reshape(leading + (columns // BLOCK, BLOCK // (2 * stride_len), 2, stride_len))
        upper_half = paired[..., 0, :]
        lower_half = paired[..., 1, :]
        blocks = jnp.stack([upper_half + lower_half, upper_half - lower_half], axis=-2)
        blocks = blocks.reshape(leading + (columns // BLOCK, BLOCK))
        stride_len = stride_len * 2
    return blocks.reshape(values.shape) * (1.0 / math.sqrt(BLOCK))

def encode_blocks(rotated):
    leading = rotated.shape[:-1]
    columns = rotated.shape[-1]
    blocks = rotated.reshape(leading + (columns // BLOCK, BLOCK))
    spread = jnp.sqrt(lax.optimization_barrier(jnp.mean(blocks * blocks, axis=-1)) + epsilon)
    block_scale = (CLIP_WIDTH * spread / CODE_LIMIT).astype(jnp.bfloat16)
    ratio = blocks / block_scale.astype(jnp.float32)[..., None]
    encoded = jnp.clip(ratio, -CODE_LIMIT, CODE_LIMIT).astype(jnp.bfloat16)
    return (encoded.reshape(rotated.shape), block_scale)

def decode_blocks(encoded, block_scale):
    leading = encoded.shape[:-1]
    columns = encoded.shape[-1]
    blocks = encoded.astype(jnp.float32).reshape(leading + (columns // BLOCK, BLOCK))
    blocks = blocks * block_scale.astype(jnp.float32)[..., None]
    return blocks.reshape(encoded.shape)

def reference(local_w, base_w, momentum):

    def add_worker(summed, local_one):
        encoded, block_scale = encode_blocks(rotate(base_w - local_one.astype(jnp.float32)))
        return (summed + rotate(decode_blocks(encoded, block_scale)), None)
    summed, _ = lax.scan(add_worker, jnp.zeros(base_w.shape, jnp.float32), local_w)
    pseudo = summed * (1.0 / WORKERS)
    new_momentum = NESTEROV_MU * momentum + pseudo
    outer_step = pseudo + NESTEROV_MU * new_momentum
    encoded, block_scale = encode_blocks(rotate(outer_step))
    new_base = base_w - OUTER_RATE * rotate(decode_blocks(encoded, block_scale))
    return (new_base, new_momentum)
```

```python
import functools
import math

import jax
import jax.numpy as jnp
from jax import lax
from jax.experimental import pallas as pl
from jax.experimental.pallas import tpu as pltpu
from jax.sharding import PartitionSpec as P

MESH = pl.DeviceIdType.MESH
F32 = jnp.float32
BF16 = jnp.bfloat16

BLOCK = 128
WORKERS = 32
EPSILON = 1e-06
CODE_LIMIT = 448.0
CLIP_WIDTH = 2.0
NESTEROV_MU = 0.9
OUTER_RATE = 0.7
ROOT = math.sqrt(BLOCK)

ZS, XS, CORES = 4, 4, 2
ROWS = 8
GROUP = 16
SHIFT = (0, -2, 1, 1)


def signs(size):
    row = lax.broadcasted_iota(jnp.int32, (size, size), 0)
    col = lax.broadcasted_iota(jnp.int32, (size, size), 1)
    common = jnp.bitwise_and(jnp.bitwise_and(row, col), BLOCK - 1)
    for shift in (4, 2, 1):
        common = jnp.bitwise_xor(common, jnp.right_shift(common, shift))
    sign = (1 - 2 * jnp.bitwise_and(common, 1)).astype(F32)
    same = jnp.right_shift(row, 7) == jnp.right_shift(col, 7)
    return jnp.where(same, sign, 0.0).astype(BF16), jnp.where(same, 1.0, 0.0).astype(BF16)


def limit_of(square_sum):
    mean = square_sum * (1.0 / BLOCK) + EPSILON
    scale = (mean * lax.rsqrt(mean) * (CLIP_WIDTH / CODE_LIMIT)).astype(BF16)
    return scale.astype(F32)


def rotate_exactly(values, table):
    high = values.astype(BF16)
    low = (values - high.astype(F32)).astype(BF16)
    return jnp.dot(high, table, preferred_element_type=F32) + jnp.dot(low, table, preferred_element_type=F32)


def kernel(
    halves,
    local_hbm, base_hbm, mom_hbm,
    out_hbm, out_mom_hbm,
    local_v, base_v, mom_v, out_v, table2, ones2,
    enc, sib, ring_a, ring_l, ring_r, zsend, zrecv, acc, gath,
    in_sem, mom_sem, out_sem, mom_out_sem,
    sib_s, sib_r, a_s, a_r, b_s, b_r, c_s, c_r, z_s, z_r,
    gz_s, gz_r, gf_s, gf_r, gh_s, gh_r, gs_s, gs_r,
):
    me = lax.axis_index("worker")
    z, x, core = me // 8, (me // 2) % 4, me % 2
    inner = lax.rem(z, 3) != 0
    zz = jnp.minimum(z, 3 - z)
    high = z // 2
    tiles = halves * 2

    def order(s):
        first = (3 - s) + zz * SHIFT[s]
        return first + high * (3 - 2 * first)

    def at(z_, x_, core_):
        return {"worker": (z_ * XS + x_) * CORES + core_}

    xr, xl, xo = (x + 1) % XS, (x + XS - 1) % XS, (x + 2) % XS
    right, left, pair = at(z, xr, core), at(z, xl, core), at(z, x, 1 - core)
    toward, away = 1 - 2 * high, 2 * high - 1

    zds = [order(s) for s in range(ZS)]
    rows_of = [pl.ds(pl.multiple_of(zd * 64, 64), 64) for zd in zds]

    def copy(src, dst, send, recv, device):
        return pltpu.make_async_remote_copy(
            src_ref=src, dst_ref=dst, send_sem=send, recv_sem=recv, device_id=device, device_id_type=MESH
        )

    loads = []
    for s in range(ZS):
        loads.append((
            pltpu.make_async_copy(base_hbm.at[rows_of[s]], base_v.at[rows_of[s]], in_sem.at[s, 0]),
            pltpu.make_async_copy(local_hbm.at[0, rows_of[s]], local_v.at[rows_of[s]], in_sem.at[s, 1]),
        ))
        for one in loads[s]:
            one.start()
    mom_load = pltpu.make_async_copy(mom_hbm, mom_v, mom_sem)
    mom_load.start()

    barrier = pltpu.get_barrier_semaphore()
    for device in (right, left, pair, at(z + toward, x, core)):
        pl.semaphore_signal(barrier, inc=1, device_id=device, device_id_type=MESH)

    @pl.when(inner)
    def _():
        pl.semaphore_signal(barrier, inc=1, device_id=at(z + away, x, core), device_id_type=MESH)

    table, ones = signs(2 * BLOCK)
    table2[...] = table
    ones2[...] = ones

    def encode(s):
        for one in loads[s]:
            one.wait()
        zd = zds[s]

        def half_loop(half, carry):
            for k in range(halves):
                cols = pl.ds(pl.multiple_of((half * halves + k) * 256, 256), 256)
                diff = base_v[rows_of[s], cols] - local_v[rows_of[s], cols].astype(F32)
                turned = jnp.dot(diff.astype(BF16), table2[...], preferred_element_type=F32)
                square = jnp.dot((diff * diff).astype(BF16), ones2[...], preferred_element_type=F32)
                limit = limit_of(square) * (CODE_LIMIT * ROOT)
                value = jnp.minimum(jnp.maximum(turned, -limit), limit)
                for xd in range(XS):
                    for c in range(CORES):
                        r = xd * GROUP + c * ROWS
                        both = jnp.concatenate(
                            [value[r : r + ROWS, :BLOCK], value[r : r + ROWS, BLOCK:]], axis=0
                        )
                        enc[c, zd, xd, half, :, pl.ds(k * BLOCK, BLOCK)] = both.astype(BF16)
            return carry

        lax.fori_loop(0, 2, half_loop, 0)

    def send_pair(s):
        c = copy(enc.at[1 - core, zds[s]], sib.at[s], sib_s.at[s], sib_r.at[s], pair)
        c.start()
        return [c]

    def add_pair(s):
        zd = zds[s]
        copy(sib.at[s], sib.at[s], sib_s.at[s], sib_r.at[s], pair).wait_recv()
        for xd in range(XS):
            for half in range(2):
                enc[core, zd, xd, half] = (
                    enc[core, zd, xd, half].astype(F32) + sib[s, xd, half].astype(F32)
                ).astype(BF16)
        sent = [
            copy(enc.at[core, zd, xo, 0], ring_a.at[s, 0], a_s.at[s, 0], a_r.at[s, 0], right),
            copy(enc.at[core, zd, xo, 1], ring_a.at[s, 1], a_s.at[s, 1], a_r.at[s, 1], left),
            copy(enc.at[core, zd, xr, 1], ring_l.at[s, 1], b_s.at[s, 0], b_r.at[s, 0], right),
            copy(enc.at[core, zd, xl, 0], ring_r.at[s, 0], b_s.at[s, 1], b_r.at[s, 1], left),
        ]
        for one in sent:
            one.start()
        return sent

    def add_far(s):
        zd = zds[s]
        sent = []
        for half, to, device, land in ((0, xr, right, ring_l), (1, xl, left, ring_r)):
            copy(ring_a.at[s, half], ring_a.at[s, half], a_s.at[s, half], a_r.at[s, half], device).wait_recv()
            enc[core, zd, to, half] = (
                enc[core, zd, to, half].astype(F32) + ring_a[s, half].astype(F32)
            ).astype(BF16)
            sent.append(copy(enc.at[core, zd, to, half], land.at[s, half], c_s.at[s, half], c_r.at[s, half], device))
            sent[-1].start()
        return sent

    def add_ring(s):
        zd = zds[s]
        copy(ring_l.at[s, 1], ring_l.at[s, 1], b_s.at[s, 0], b_r.at[s, 0], right).wait_recv()
        copy(ring_r.at[s, 0], ring_r.at[s, 0], b_s.at[s, 1], b_r.at[s, 1], left).wait_recv()
        copy(ring_l.at[s, 0], ring_l.at[s, 0], c_s.at[s, 0], c_r.at[s, 0], right).wait_recv()
        copy(ring_r.at[s, 1], ring_r.at[s, 1], c_s.at[s, 1], c_r.at[s, 1], left).wait_recv()

        def total(half):
            return (
                enc[core, zd, x, half].astype(F32) + ring_l[s, half].astype(F32) + ring_r[s, half].astype(F32)
            )

        def arrived(which, way):
            copy(zrecv.at[which, way], zrecv.at[which, way], z_s.at[0], z_r.at[which, way], pair).wait_recv()

        if s < ZS - 1:
            way = (zd < z).astype(jnp.int32)

            @pl.when(inner)
            def _():
                arrived(zd, way)
                for half in range(2):
                    zsend[s, half] = (total(half) + zrecv[zd, way, half].astype(F32)).astype(BF16)

            @pl.when(jnp.logical_not(inner))
            def _():
                for half in range(2):
                    zsend[s, half] = total(half).astype(BF16)

            c = copy(zsend.at[s], zrecv.at[zd, way], z_s.at[s], z_r.at[zd, way], at(z + 1 - 2 * way, x, core))
            c.start()
            return [c]

        for half in range(2):
            acc[half] = total(half)
        for way, there in ((0, z > 0), (1, z < ZS - 1)):

            @pl.when(there)
            def _():
                arrived(z, way)
                for half in range(2):
                    acc[half] += zrecv[z, way, half].astype(F32)

        return []

    sends = []
    encode(0)
    pl.semaphore_wait(barrier, 4 + inner.astype(jnp.int32))
    sends += send_pair(0)
    encode(1)
    sends += send_pair(1)
    sends += add_pair(0)
    encode(2)
    sends += send_pair(2)
    sends += add_far(0)
    sends += add_pair(1)
    encode(3)
    sends += send_pair(3)
    sends += add_far(1)
    sends += add_pair(2)
    sends += add_ring(0)
    sends += add_far(2)
    sends += add_pair(3)
    sends += add_ring(1)
    sends += add_far(3)
    sends += add_ring(2)
    mom_load.wait()
    sends += add_ring(3)

    table1 = table2[:BLOCK, :BLOCK]

    def stacked(read):
        return jnp.concatenate([read(k) for k in range(tiles)], axis=0)

    def cut(array, k):
        return array[k * GROUP : (k + 1) * GROUP]

    total = stacked(lambda k: acc[k // halves, :, (k % halves) * BLOCK : (k % halves + 1) * BLOCK])
    momentum = stacked(
        lambda k: jnp.concatenate(
            [mom_v[:, 256 * k : 256 * k + BLOCK], mom_v[:, 256 * k + BLOCK : 256 * (k + 1)]], axis=0
        )
    )
    pseudo = rotate_exactly(total, table1) * (1.0 / (BLOCK * WORKERS))
    new_momentum = NESTEROV_MU * momentum + pseudo
    for k in range(tiles):
        one = cut(new_momentum, k)
        mom_v[:, 256 * k : 256 * k + BLOCK] = one[:ROWS]
        mom_v[:, 256 * k + BLOCK : 256 * (k + 1)] = one[ROWS:]
    mom_store = pltpu.make_async_copy(mom_v, out_mom_hbm, mom_out_sem)
    mom_store.start()
    outer_step = pseudo + NESTEROV_MU * new_momentum
    square = jnp.sum(outer_step * outer_step, axis=-1, keepdims=True)
    limit = limit_of(square) * CODE_LIMIT
    turned = rotate_exactly(outer_step, table1) * (1.0 / ROOT)
    value = jnp.minimum(jnp.maximum(turned, -limit), limit).astype(BF16)
    for k in range(tiles):
        gath[core, z, x, k // halves, :, (k % halves) * BLOCK : (k % halves + 1) * BLOCK] = cut(value, k)

    zos = [zds[ZS - 1 - s] for s in range(ZS)]

    def own_z():
        c = copy(gath.at[core, z, x], gath.at[core, z, x], gz_s.at[0], gz_r.at[z], at(z + toward, x, core))
        c.start()

        @pl.when(inner)
        def _():
            copy(gath.at[core, z, x], gath.at[core, z, x], gz_s.at[4], gz_r.at[z], at(z + away, x, core)).start()

        return [c]

    def next_z(s):
        zo = zos[s]
        spot = gath.at[core, zo, x]
        copy(spot, spot, gz_s.at[s], gz_r.at[zo], pair).wait_recv()

        @pl.when(inner)
        def _():
            to = z + 2 * (zo < z).astype(jnp.int32) - 1
            copy(spot, spot, gz_s.at[s], gz_r.at[zo], at(to, x, core)).start()

    def to_pair(s, i, x_):
        spot = gath.at[core, zos[s], x_]
        c = copy(spot, spot, gs_s.at[s, i], gs_r.at[s, i], pair)
        c.start()
        return [c]

    def full(s):
        spot = gath.at[core, zos[s], x]
        sent = [
            copy(spot, spot, gf_s.at[s, 0], gf_r.at[s, 0], right),
            copy(spot, spot, gf_s.at[s, 1], gf_r.at[s, 1], left),
        ]
        for one in sent:
            one.start()
        return sent + to_pair(s, 0, x)

    def onward(s):
        sent = []
        for half, x_, device in ((0, xl, right), (1, xr, left)):
            spot = gath.at[core, zos[s], x_]
            copy(spot, spot, gf_s.at[s, half], gf_r.at[s, half], device).wait_recv()
            sent.append(copy(spot.at[half], spot.at[half], gh_s.at[s, half], gh_r.at[s, half], device))
            sent[-1].start()
            sent += to_pair(s, 1 + half, x_)
        return sent

    def far(s):
        spot = gath.at[core, zos[s], xo]
        for half in range(2):
            copy(spot.at[half], spot.at[half], gh_s.at[s, half], gh_r.at[s, half], pair).wait_recv()
        return to_pair(s, 3, xo)

    def decode(s, c, x_):
        zo = zos[s]
        rows = pl.ds(pl.multiple_of((zo * XS + x_) * GROUP + c * ROWS, ROWS), ROWS)
        codes = stacked(lambda k: gath[c, zo, x_, k // halves, :, (k % halves) * BLOCK : (k % halves + 1) * BLOCK])
        back = jnp.dot(codes, table1, preferred_element_type=F32) * (OUTER_RATE / ROOT)
        for k in range(tiles):
            one = cut(back, k)
            for b in range(2):
                cols = slice(256 * k + b * BLOCK, 256 * k + (b + 1) * BLOCK)
                out_v[rows, cols] = base_v[rows, cols] - one[b * ROWS : (b + 1) * ROWS]

    def finish(s):
        zo = zos[s]

        def mine(x_, carry):
            decode(s, core, x_)
            return carry

        lax.fori_loop(0, XS, mine, 0)
        for i, x_ in enumerate((x, xl, xr, xo)):
            spot = gath.at[1 - core, zo, x_]
            copy(spot, spot, gs_s.at[s, i], gs_r.at[s, i], pair).wait_recv()

        def others(x_, carry):
            decode(s, 1 - core, x_)
            return carry

        lax.fori_loop(0, XS, others, 0)
        rows = rows_of[ZS - 1 - s]
        store = pltpu.make_async_copy(out_v.at[rows], out_hbm.at[rows], out_sem.at[s])
        store.start()
        return store

    stores = []
    sends += own_z()
    sends += full(0)
    next_z(1)
    sends += full(1)
    sends += onward(0)
    next_z(2)
    sends += full(2)
    sends += onward(1)
    sends += far(0)
    stores.append(finish(0))
    next_z(3)
    sends += full(3)
    sends += onward(2)
    sends += far(1)
    stores.append(finish(1))
    sends += onward(3)
    sends += far(2)
    stores.append(finish(2))
    sends += far(3)
    stores.append(finish(3))

    for one in sends:
        one.wait_send()

    @pl.when(inner)
    def _():
        for i in range(1, 5):
            spot = gath.at[core, z, x]
            copy(spot, spot, gz_s.at[i], gz_r.at[z], pair).wait_send()

    for store in stores:
        store.wait()
    mom_store.wait()


def step(local_w, base_w, momentum):
    rows, columns = base_w.shape
    halves = columns // 512
    width = halves * BLOCK
    dma = pltpu.SemaphoreType.DMA
    chunk = (2, GROUP, width)
    return pl.pallas_call(
        functools.partial(kernel, halves),
        out_shape=(
            jax.ShapeDtypeStruct(base_w.shape, F32),
            jax.ShapeDtypeStruct(momentum.shape, F32),
        ),
        in_specs=[pl.BlockSpec(memory_space=pl.ANY)] * 3,
        out_specs=[pl.BlockSpec(memory_space=pl.ANY)] * 2,
        scratch_shapes=[
            pltpu.VMEM((rows, columns), BF16),
            pltpu.VMEM((rows, columns), F32),
            pltpu.VMEM((ROWS, columns), F32),
            pltpu.VMEM((rows, columns), F32),
            pltpu.VMEM((2 * BLOCK, 2 * BLOCK), BF16),
            pltpu.VMEM((2 * BLOCK, 2 * BLOCK), BF16),
            pltpu.VMEM((CORES, ZS, XS) + chunk, BF16),
            pltpu.VMEM((ZS, XS) + chunk, BF16),
            pltpu.VMEM((ZS,) + chunk, BF16),
            pltpu.VMEM((ZS,) + chunk, BF16),
            pltpu.VMEM((ZS,) + chunk, BF16),
            pltpu.VMEM((ZS - 1,) + chunk, BF16),
            pltpu.VMEM((ZS, 2) + chunk, BF16),
            pltpu.VMEM(chunk, F32),
            pltpu.VMEM((CORES, ZS, XS) + chunk, BF16),
            dma((ZS, 2)), dma, dma((ZS,)), dma,
            dma((ZS,)), dma((ZS,)),
            dma((ZS, 2)), dma((ZS, 2)),
            dma((ZS, 2)), dma((ZS, 2)),
            dma((ZS, 2)), dma((ZS, 2)),
            dma((ZS - 1,)), dma((ZS, 2)),
            dma((5,)), dma((ZS,)),
            dma((ZS, 2)), dma((ZS, 2)),
            dma((ZS, 2)), dma((ZS, 2)),
            dma((ZS, 4)), dma((ZS, 4)),
        ],
        compiler_params=pltpu.CompilerParams(
            collective_id=0, has_side_effects=True, vmem_limit_bytes=60 * 1024 * 1024
        ),
    )(local_w, base_w, momentum)


def solution(mesh):
    in_specs = (P("worker", "shard", None), P("shard", None), P(("shard", "worker"), None))
    out_specs = (P("shard", None), P(("shard", "worker"), None))
    return jax.shard_map(step, mesh=mesh, in_specs=in_specs, out_specs=out_specs, check_vma=False)
```

```python
import functools
import math

import jax
import jax.numpy as jnp
from jax import lax
from jax.experimental import pallas as pl
from jax.experimental.pallas import tpu as pltpu
from jax.sharding import PartitionSpec as P

MESH = pl.DeviceIdType.MESH
F32 = jnp.float32
BF16 = jnp.bfloat16

BLOCK = 128
WORKERS = 32
EPSILON = 1e-06
CODE_LIMIT = 448.0
CLIP_WIDTH = 2.0
NESTEROV_MU = 0.9
OUTER_RATE = 0.7
ROOT = math.sqrt(BLOCK)

ZS, XS, CORES, PIECES = 4, 4, 2, 6
ROWS = 8
GROUP = 16
STRAIGHT_IN = (0, 1, 2, 3, 4, 5)
STRAIGHT_OUT = (0, 1, 2, 3, 4, 5)


def signs(size):
    row = lax.broadcasted_iota(jnp.int32, (size, size), 0)
    col = lax.broadcasted_iota(jnp.int32, (size, size), 1)
    common = jnp.bitwise_and(jnp.bitwise_and(row, col), BLOCK - 1)
    for shift in (4, 2, 1):
        common = jnp.bitwise_xor(common, jnp.right_shift(common, shift))
    sign = (1 - 2 * jnp.bitwise_and(common, 1)).astype(F32)
    same = jnp.right_shift(row, 7) == jnp.right_shift(col, 7)
    return jnp.where(same, sign, 0.0).astype(BF16), jnp.where(same, 1.0, 0.0).astype(BF16)


def limit_of(square_sum):
    mean = square_sum * (1.0 / BLOCK) + EPSILON
    scale = (mean * lax.rsqrt(mean) * (CLIP_WIDTH / CODE_LIMIT)).astype(BF16)
    return scale.astype(F32)


def rotate_exactly(values, table):
    high = values.astype(BF16)
    low = (values - high.astype(F32)).astype(BF16)
    return jnp.dot(high, table, preferred_element_type=F32) + jnp.dot(low, table, preferred_element_type=F32)


def kernel(
    tiles,
    local_hbm, base_hbm, mom_hbm,
    out_v, out_mom,
    local_v, base_v, mom_v, table2, ones2,
    enc, sib, ring_a, ring_c, ring_d, zsend, zrecv, acc, gath,
    in_sem, mom_sem,
    sib_s, sib_r, a_s, a_r, c_s, c_r, d_s, d_r, z_s, z_r,
    gz_s, gz_r, gf_s, gf_r, gh_s, gh_r, gp_s, gp_r,
):
    me = lax.axis_index("worker")
    z, x, core = me // 8, (me // 2) % 4, me % 2
    def at(z_, x_, core_):
        return {"worker": (z_ * XS + x_) * CORES + core_}

    xr, xl, xo = (x + 1) % XS, (x + XS - 1) % XS, (x + 2) % XS
    right, left, across, pair = at(z, xr, core), at(z, xl, core), at(z, xo, core), at(z, x, 1 - core)
    others = [(z + i) % ZS for i in range(1, ZS)]
    width = tiles * 2 * BLOCK

    def copy(src, dst, send, recv, device):
        return pltpu.make_async_remote_copy(
            src_ref=src, dst_ref=dst, send_sem=send, recv_sem=recv, device_id=device, device_id_type=MESH
        )

    sent = []

    def start(*args):
        one = copy(*args)
        one.start()
        sent.append(one)

    def arrived(spot, send, recv):
        copy(spot, spot, send, recv, pair).wait_recv()

    loads = []
    for k in range(PIECES):
        cols = pl.ds(k * width, width)
        loads.append((
            pltpu.make_async_copy(base_hbm.at[:, cols], base_v.at[:, cols], in_sem.at[k, 0]),
            pltpu.make_async_copy(local_hbm.at[0, :, cols], local_v.at[:, cols], in_sem.at[k, 1]),
        ))
        for one in loads[k]:
            one.start()
    mom_load = pltpu.make_async_copy(mom_hbm, mom_v, mom_sem)
    mom_load.start()

    barrier = pltpu.get_barrier_semaphore()
    greeted = [right, left, across, pair] + [at(zd, x, core) for zd in others]
    for device in greeted:
        pl.semaphore_signal(barrier, inc=1, device_id=device, device_id_type=MESH)

    table, ones = signs(2 * BLOCK)
    table2[...] = table
    ones2[...] = ones

    def enter():
        pl.semaphore_wait(barrier, len(greeted))

    def sides(k):
        return (xr, right, xl, left) if k % 2 == 0 else (xl, left, xr, right)

    def encode(k):
        for one in loads[k]:
            one.wait()
        for zd in range(ZS):
            rows = slice(zd * XS * GROUP, (zd + 1) * XS * GROUP)
            for t in range(tiles):
                cols = slice((k * tiles + t) * 256, (k * tiles + t + 1) * 256)
                diff = base_v[rows, cols] - local_v[rows, cols].astype(F32)
                turned = jnp.dot(diff.astype(BF16), table2[...], preferred_element_type=F32)
                square = jnp.dot((diff * diff).astype(BF16), ones2[...], preferred_element_type=F32)
                limit = limit_of(square) * (CODE_LIMIT * ROOT)
                value = jnp.minimum(jnp.maximum(turned, -limit), limit)
                for xd in range(XS):
                    for c in range(CORES):
                        r = xd * GROUP + c * ROWS
                        both = jnp.concatenate([value[r : r + ROWS, :BLOCK], value[r : r + ROWS, BLOCK:]], axis=0)
                        enc[c, k, xd, zd, :, t * BLOCK : (t + 1) * BLOCK] = both.astype(BF16)

    def send_pair(k):
        start(enc.at[1 - core, k], sib.at[k], sib_s.at[k], sib_r.at[k], pair)

    def add_pair(k):
        arrived(sib.at[k], sib_s.at[k], sib_r.at[k])
        xv, via, xw, other = sides(k)
        straight = k in STRAIGHT_IN
        for xd in (xo, xw, xv, x):
            enc[core, k, xd] = (enc[core, k, xd].astype(F32) + sib[k, xd].astype(F32)).astype(BF16)
            if xd is xo:
                start(enc.at[core, k, xo], ring_a.at[k], a_s.at[k], a_r.at[k], across if straight else via)
            elif xd is xw:
                start(enc.at[core, k, xw], ring_d.at[k], d_s.at[k], d_r.at[k], other)
            elif xd is xv and straight:
                start(enc.at[core, k, xv], ring_c.at[k], c_s.at[k], c_r.at[k], via)

    def add_far(k):
        xv, via, _, _ = sides(k)
        arrived(ring_a.at[k], a_s.at[k], a_r.at[k])
        enc[core, k, xv] = (enc[core, k, xv].astype(F32) + ring_a[k].astype(F32)).astype(BF16)
        start(enc.at[core, k, xv], ring_c.at[k], c_s.at[k], c_r.at[k], via)

    def add_ring(k):
        arrived(ring_d.at[k], d_s.at[k], d_r.at[k])
        arrived(ring_c.at[k], c_s.at[k], c_r.at[k])
        if k in STRAIGHT_IN:
            arrived(ring_a.at[k], a_s.at[k], a_r.at[k])

        def total(zd):
            here = enc[core, k, x, zd].astype(F32) + ring_c[k, zd].astype(F32) + ring_d[k, zd].astype(F32)
            return here + ring_a[k, zd].astype(F32) if k in STRAIGHT_IN else here

        for i, zd in enumerate(others):
            zsend[k, i] = total(zd).astype(BF16)
            start(zsend.at[k, i], zrecv.at[k, z], z_s.at[k, i], z_r.at[k, z], at(zd, x, core))
        acc[k] = total(z)

    def stacked(read):
        return jnp.concatenate([read(t) for t in range(tiles)], axis=0)

    def cut(array, t):
        return array[t * GROUP : (t + 1) * GROUP]

    def own(k):
        if k == 0:
            mom_load.wait()
        table1 = table2[:BLOCK, :BLOCK]
        summed = acc[k]
        for zs in others:
            arrived(zrecv.at[k, zs], z_s.at[k, 0], z_r.at[k, zs])
            summed = summed + zrecv[k, zs].astype(F32)
        total = stacked(lambda t: summed[:, t * BLOCK : (t + 1) * BLOCK])
        first = k * width
        momentum = stacked(
            lambda t: jnp.concatenate(
                [mom_v[:, first + b * BLOCK : first + (b + 1) * BLOCK] for b in (2 * t, 2 * t + 1)], axis=0
            )
        )
        pseudo = rotate_exactly(total, table1) * (1.0 / (BLOCK * WORKERS))
        new_momentum = NESTEROV_MU * momentum + pseudo
        outer_step = pseudo + NESTEROV_MU * new_momentum
        square = jnp.sum(outer_step * outer_step, axis=-1, keepdims=True)
        limit = limit_of(square) * CODE_LIMIT
        turned = rotate_exactly(outer_step, table1) * (1.0 / ROOT)
        value = jnp.minimum(jnp.maximum(turned, -limit), limit).astype(BF16)
        for t in range(tiles):
            gath[core, k, x, z, :, t * BLOCK : (t + 1) * BLOCK] = cut(value, t)
        spot = gath.at[core, k, x, z]
        for i, zd in enumerate(others):
            start(spot, spot, gz_s.at[k, i], gz_r.at[k, z], at(zd, x, core))
        for t in range(tiles):
            for b in range(2):
                cols = slice(first + (2 * t + b) * BLOCK, first + (2 * t + b + 1) * BLOCK)
                out_mom[:, cols] = cut(new_momentum, t)[b * ROWS : (b + 1) * ROWS]

    def to_pair(k, i, x_):
        spot = gath.at[core, k, x_]
        start(spot, spot, gp_s.at[k, i], gp_r.at[k, i], pair)

    def full(k):
        for zo in others:
            arrived(gath.at[core, k, x, zo], gz_s.at[k, 0], gz_r.at[k, zo])
        spot = gath.at[core, k, x]
        if k in STRAIGHT_OUT:
            start(spot, spot, gh_s.at[k], gh_r.at[k], across)
        start(spot, spot, gf_s.at[k, 0], gf_r.at[k, 0], right)
        start(spot, spot, gf_s.at[k, 1], gf_r.at[k, 1], left)
        to_pair(k, 0, x)

    def onward(k):
        ways = ((0, xl, right), (1, xr, left))
        for i, x_, device in ways if k % 2 == 0 else ways[::-1]:
            spot = gath.at[core, k, x_]
            arrived(spot, gf_s.at[k, i], gf_r.at[k, i])
            if i == k % 2 and k not in STRAIGHT_OUT:
                start(spot, spot, gh_s.at[k], gh_r.at[k], device)
            to_pair(k, 1 + i, x_)

    def far(k):
        arrived(gath.at[core, k, xo], gh_s.at[k], gh_r.at[k])
        to_pair(k, 3, xo)

    def decode(k, c, x_):
        table1 = table2[:BLOCK, :BLOCK]
        codes = jnp.concatenate(
            [stacked(lambda t: gath[c, k, x_, zo, :, t * BLOCK : (t + 1) * BLOCK]) for zo in range(ZS)], axis=0
        )
        back = jnp.dot(codes, table1, preferred_element_type=F32) * (OUTER_RATE / ROOT)
        for zo in range(ZS):
            rows = pl.ds(pl.multiple_of((zo * XS + x_) * GROUP + c * ROWS, ROWS), ROWS)
            for t in range(tiles):
                for b in range(2):
                    first = k * width + (2 * t + b) * BLOCK
                    cols = slice(first, first + BLOCK)
                    out_v[rows, cols] = base_v[rows, cols] - cut(back, zo * tiles + t)[b * ROWS : (b + 1) * ROWS]

    def finish(k):
        for x_ in (x, xl, xr, xo):
            decode(k, core, x_)
        for i, x_ in enumerate((x, xl, xr, xo)):
            arrived(gath.at[1 - core, k, x_], gp_s.at[k, i], gp_r.at[k, i])
            decode(k, 1 - core, x_)

    plan = (
        (encode, 0), (encode, 1), (encode, 2), (encode, 3), (encode, 4), (encode, 5), (enter,), (send_pair, 0),
        (send_pair, 1), (send_pair, 2), (send_pair, 3), (send_pair, 4), (send_pair, 5), (add_pair, 0), (add_pair, 1),
        (add_pair, 2), (add_pair, 3), (add_pair, 4), (add_pair, 5), (add_ring, 0), (add_ring, 1), (add_ring, 2),
        (own, 0), (add_ring, 3), (own, 1), (add_ring, 4), (own, 2), (full, 0), (add_ring, 5), (own, 3), (full, 1),
        (own, 4), (full, 2), (onward, 0), (far, 0), (own, 5), (finish, 0), (full, 3), (onward, 1), (far, 1), (full, 4),
        (finish, 1), (onward, 2), (far, 2), (full, 5), (finish, 2), (onward, 3), (far, 3), (finish, 3), (onward, 4),
        (far, 4), (finish, 4), (onward, 5), (far, 5), (finish, 5),
    )
    for act, *which in plan:
        act(*which)

    for one in sent:
        one.wait_send()


def step(local_w, base_w, momentum):
    rows, columns = base_w.shape
    tiles = columns // (256 * PIECES)
    dma = pltpu.SemaphoreType.DMA
    chunk = (GROUP, tiles * BLOCK)
    ring = (PIECES, ZS) + chunk
    held = (CORES, PIECES, XS, ZS) + chunk
    each = dma((PIECES,))
    return pl.pallas_call(
        functools.partial(kernel, tiles),
        out_shape=(pltpu.VMEM(base_w.shape, F32), pltpu.VMEM(momentum.shape, F32)),
        in_specs=[pl.BlockSpec(memory_space=pl.ANY)] * 3,
        out_specs=[pl.BlockSpec(memory_space=pltpu.VMEM)] * 2,
        scratch_shapes=[
            pltpu.VMEM((rows, columns), BF16),
            pltpu.VMEM((rows, columns), F32),
            pltpu.VMEM((ROWS, columns), F32),
            pltpu.VMEM((2 * BLOCK, 2 * BLOCK), BF16),
            pltpu.VMEM((2 * BLOCK, 2 * BLOCK), BF16),
            pltpu.VMEM(held, BF16),
            pltpu.VMEM((PIECES, XS, ZS) + chunk, BF16),
            pltpu.VMEM(ring, BF16),
            pltpu.VMEM(ring, BF16),
            pltpu.VMEM(ring, BF16),
            pltpu.VMEM((PIECES, ZS - 1) + chunk, BF16),
            pltpu.VMEM(ring, BF16),
            pltpu.VMEM((PIECES,) + chunk, F32),
            pltpu.VMEM(held, BF16),
            dma((PIECES, 2)), dma,
            each, each, each, each, each, each, each, each,
            dma((PIECES, ZS - 1)), dma((PIECES, ZS)),
            dma((PIECES, ZS - 1)), dma((PIECES, ZS)),
            dma((PIECES, 2)), dma((PIECES, 2)),
            each, each,
            dma((PIECES, 4)), dma((PIECES, 4)),
        ],
        compiler_params=pltpu.CompilerParams(
            collective_id=0, has_side_effects=True, vmem_limit_bytes=50 * 1024 * 1024
        ),
    )(*(pltpu.with_memory_space_constraint(a, pltpu.HBM) for a in (local_w, base_w, momentum)))


def solution(mesh):
    in_specs = (P("worker", "shard", None), P("shard", None), P(("shard", "worker"), None))
    out_specs = (P("shard", None), P(("shard", "worker"), None))
    return jax.shard_map(step, mesh=mesh, in_specs=in_specs, out_specs=out_specs, check_vma=False)
```

```python
import functools
import math

import jax
import jax.numpy as jnp
from jax import lax
from jax.experimental import pallas as pl
from jax.experimental.pallas import tpu as pltpu
from jax.sharding import PartitionSpec as P

MESH = pl.DeviceIdType.MESH
F32 = jnp.float32
BF16 = jnp.bfloat16

BLOCK = 128
WORKERS = 32
EPSILON = 1e-06
CODE_LIMIT = 448.0
CLIP_WIDTH = 2.0
NESTEROV_MU = 0.9
OUTER_RATE = 0.7
ROOT = math.sqrt(BLOCK)

ZS, XS, CORES, PIECES = 4, 4, 2, 6
ROWS = 8
GROUP = 16
STRAIGHT_IN = (0, 1, 2, 3, 4, 5)
STRAIGHT_OUT = (0, 1, 2, 3, 4, 5)


def signs(size):
    row = lax.broadcasted_iota(jnp.int32, (size, size), 0)
    col = lax.broadcasted_iota(jnp.int32, (size, size), 1)
    common = jnp.bitwise_and(jnp.bitwise_and(row, col), BLOCK - 1)
    for shift in (4, 2, 1):
        common = jnp.bitwise_xor(common, jnp.right_shift(common, shift))
    sign = (1 - 2 * jnp.bitwise_and(common, 1)).astype(F32)
    same = jnp.right_shift(row, 7) == jnp.right_shift(col, 7)
    return jnp.where(same, sign, 0.0).astype(BF16), jnp.where(same, 1.0, 0.0).astype(BF16)


def limit_of(square_sum):
    mean = square_sum * (1.0 / BLOCK) + EPSILON
    scale = (mean * lax.rsqrt(mean) * (CLIP_WIDTH / CODE_LIMIT)).astype(BF16)
    return scale.astype(F32)


def rotate_exactly(values, table):
    high = values.astype(BF16)
    low = (values - high.astype(F32)).astype(BF16)
    return jnp.dot(high, table, preferred_element_type=F32) + jnp.dot(low, table, preferred_element_type=F32)


def kernel(
    tiles,
    local_hbm, base_hbm, mom_hbm,
    out_v, out_mom,
    local_v, base_v, mom_v, table2, ones2,
    enc, sib, ring_a, ring_c, ring_d, zsend, zrecv, acc, gath,
    in_sem, mom_sem,
    sib_s, sib_r, a_s, a_r, c_s, c_r, d_s, d_r, z_s, z_r,
    gz_s, gz_r, gf_s, gf_r, gh_s, gh_r, gp_s, gp_r,
):
    me = lax.axis_index("worker")
    z, x, core = me // 8, (me // 2) % 4, me % 2
    def at(z_, x_, core_):
        return {"worker": (z_ * XS + x_) * CORES + core_}

    xr, xl, xo = (x + 1) % XS, (x + XS - 1) % XS, (x + 2) % XS
    right, left, across, pair = at(z, xr, core), at(z, xl, core), at(z, xo, core), at(z, x, 1 - core)
    others = [(z + i) % ZS for i in range(1, ZS)]
    width = tiles * 2 * BLOCK

    def copy(src, dst, send, recv, device):
        return pltpu.make_async_remote_copy(
            src_ref=src, dst_ref=dst, send_sem=send, recv_sem=recv, device_id=device, device_id_type=MESH
        )

    sent = []

    def start(*args):
        one = copy(*args)
        one.start()
        sent.append(one)

    def arrived(spot, send, recv):
        copy(spot, spot, send, recv, pair).wait_recv()

    loads = []
    for k in range(PIECES):
        cols = pl.ds(k * width, width)
        loads.append((
            pltpu.make_async_copy(base_hbm.at[:, cols], base_v.at[:, cols], in_sem.at[k, 0]),
            pltpu.make_async_copy(local_hbm.at[0, :, cols], local_v.at[:, cols], in_sem.at[k, 1]),
        ))
        for one in loads[k]:
            one.start()
    mom_load = pltpu.make_async_copy(mom_hbm, mom_v, mom_sem)
    mom_load.start()

    barrier = pltpu.get_barrier_semaphore()
    greeted = [right, left, across, pair] + [at(zd, x, core) for zd in others]
    for device in greeted:
        pl.semaphore_signal(barrier, inc=1, device_id=device, device_id_type=MESH)

    table, ones = signs(2 * BLOCK)
    table2[...] = table
    ones2[...] = ones

    def enter():
        pl.semaphore_wait(barrier, len(greeted))

    def sides(k):
        return (xr, right, xl, left) if k % 2 == 0 else (xl, left, xr, right)

    def encode(k):
        for one in loads[k]:
            one.wait()
        for zd in range(ZS):
            rows = slice(zd * XS * GROUP, (zd + 1) * XS * GROUP)
            for t in range(tiles):
                cols = slice((k * tiles + t) * 256, (k * tiles + t + 1) * 256)
                diff = base_v[rows, cols] - local_v[rows, cols].astype(F32)
                turned = jnp.dot(diff.astype(BF16), table2[...], preferred_element_type=F32)
                square = jnp.dot((diff * diff).astype(BF16), ones2[...], preferred_element_type=F32)
                limit = limit_of(square) * (CODE_LIMIT * ROOT)
                value = jnp.minimum(jnp.maximum(turned, -limit), limit)
                for xd in range(XS):
                    for c in range(CORES):
                        r = xd * GROUP + c * ROWS
                        both = jnp.concatenate([value[r : r + ROWS, :BLOCK], value[r : r + ROWS, BLOCK:]], axis=0)
                        enc[c, k, xd, zd, :, t * BLOCK : (t + 1) * BLOCK] = both.astype(BF16)

    def send_pair(k):
        start(enc.at[1 - core, k], sib.at[k], sib_s.at[k], sib_r.at[k], pair)

    def add_pair(k):
        arrived(sib.at[k], sib_s.at[k], sib_r.at[k])
        xv, via, xw, other = sides(k)
        straight = k in STRAIGHT_IN
        for xd in (xo, xw, xv, x):
            enc[core, k, xd] = (enc[core, k, xd].astype(F32) + sib[k, xd].astype(F32)).astype(BF16)
            if xd is xo:
                start(enc.at[core, k, xo], ring_a.at[k], a_s.at[k], a_r.at[k], across if straight else via)
            elif xd is xw:
                start(enc.at[core, k, xw], ring_d.at[k], d_s.at[k], d_r.at[k], other)
            elif xd is xv and straight:
                start(enc.at[core, k, xv], ring_c.at[k], c_s.at[k], c_r.at[k], via)

    def add_far(k):
        xv, via, _, _ = sides(k)
        arrived(ring_a.at[k], a_s.at[k], a_r.at[k])
        enc[core, k, xv] = (enc[core, k, xv].astype(F32) + ring_a[k].astype(F32)).astype(BF16)
        start(enc.at[core, k, xv], ring_c.at[k], c_s.at[k], c_r.at[k], via)

    def add_ring(k):
        arrived(ring_d.at[k], d_s.at[k], d_r.at[k])
        arrived(ring_c.at[k], c_s.at[k], c_r.at[k])
        if k in STRAIGHT_IN:
            arrived(ring_a.at[k], a_s.at[k], a_r.at[k])

        def total(zd):
            here = enc[core, k, x, zd].astype(F32) + ring_c[k, zd].astype(F32) + ring_d[k, zd].astype(F32)
            return here + ring_a[k, zd].astype(F32) if k in STRAIGHT_IN else here

        for i, zd in enumerate(others):
            zsend[k, i] = total(zd).astype(BF16)
            start(zsend.at[k, i], zrecv.at[k, z], z_s.at[k, i], z_r.at[k, z], at(zd, x, core))
        acc[k] = total(z)

    def stacked(read):
        return jnp.concatenate([read(t) for t in range(tiles)], axis=0)

    def cut(array, t):
        return array[t * GROUP : (t + 1) * GROUP]

    def own(k):
        if k == 0:
            mom_load.wait()
        table1 = table2[:BLOCK, :BLOCK]
        summed = acc[k]
        for zs in others:
            arrived(zrecv.at[k, zs], z_s.at[k, 0], z_r.at[k, zs])
            summed = summed + zrecv[k, zs].astype(F32)
        total = stacked(lambda t: summed[:, t * BLOCK : (t + 1) * BLOCK])
        first = k * width
        momentum = stacked(
            lambda t: jnp.concatenate(
                [mom_v[:, first + b * BLOCK : first + (b + 1) * BLOCK] for b in (2 * t, 2 * t + 1)], axis=0
            )
        )
        pseudo = rotate_exactly(total, table1) * (1.0 / (BLOCK * WORKERS))
        new_momentum = NESTEROV_MU * momentum + pseudo
        outer_step = pseudo + NESTEROV_MU * new_momentum
        square = jnp.sum(outer_step * outer_step, axis=-1, keepdims=True)
        limit = limit_of(square) * CODE_LIMIT
        turned = rotate_exactly(outer_step, table1) * (1.0 / ROOT)
        value = jnp.minimum(jnp.maximum(turned, -limit), limit).astype(BF16)
        for t in range(tiles):
            gath[core, k, x, z, :, t * BLOCK : (t + 1) * BLOCK] = cut(value, t)
        spot = gath.at[core, k, x, z]
        for i, zd in enumerate(others):
            start(spot, spot, gz_s.at[k, i], gz_r.at[k, z], at(zd, x, core))
        for t in range(tiles):
            for b in range(2):
                cols = slice(first + (2 * t + b) * BLOCK, first + (2 * t + b + 1) * BLOCK)
                out_mom[:, cols] = cut(new_momentum, t)[b * ROWS : (b + 1) * ROWS]

    def to_pair(k, i, x_):
        spot = gath.at[core, k, x_]
        start(spot, spot, gp_s.at[k, i], gp_r.at[k, i], pair)

    def full(k):
        for zo in others:
            arrived(gath.at[core, k, x, zo], gz_s.at[k, 0], gz_r.at[k, zo])
        spot = gath.at[core, k, x]
        if k in STRAIGHT_OUT:
            start(spot, spot, gh_s.at[k], gh_r.at[k], across)
        start(spot, spot, gf_s.at[k, 0], gf_r.at[k, 0], right)
        start(spot, spot, gf_s.at[k, 1], gf_r.at[k, 1], left)
        to_pair(k, 0, x)

    def onward(k):
        ways = ((0, xl, right), (1, xr, left))
        for i, x_, device in ways if k % 2 == 0 else ways[::-1]:
            spot = gath.at[core, k, x_]
            arrived(spot, gf_s.at[k, i], gf_r.at[k, i])
            if i == k % 2 and k not in STRAIGHT_OUT:
                start(spot, spot, gh_s.at[k], gh_r.at[k], device)
            to_pair(k, 1 + i, x_)

    def far(k):
        arrived(gath.at[core, k, xo], gh_s.at[k], gh_r.at[k])
        to_pair(k, 3, xo)

    def decode(k, c, x_):
        table1 = table2[:BLOCK, :BLOCK]
        codes = jnp.concatenate(
            [stacked(lambda t: gath[c, k, x_, zo, :, t * BLOCK : (t + 1) * BLOCK]) for zo in range(ZS)], axis=0
        )
        back = jnp.dot(codes, table1, preferred_element_type=F32) * (OUTER_RATE / ROOT)
        for zo in range(ZS):
            rows = pl.ds(pl.multiple_of((zo * XS + x_) * GROUP + c * ROWS, ROWS), ROWS)
            for t in range(tiles):
                for b in range(2):
                    first = k * width + (2 * t + b) * BLOCK
                    cols = slice(first, first + BLOCK)
                    out_v[rows, cols] = base_v[rows, cols] - cut(back, zo * tiles + t)[b * ROWS : (b + 1) * ROWS]

    def finish(k):
        for x_ in (x, xl, xr, xo):
            decode(k, core, x_)
        for i, x_ in enumerate((x, xl, xr, xo)):
            arrived(gath.at[1 - core, k, x_], gp_s.at[k, i], gp_r.at[k, i])
            decode(k, 1 - core, x_)

    plan = (
        (encode, 0), (enter,), (send_pair, 0), (encode, 1), (send_pair, 1), (encode, 2), (send_pair, 2), (encode, 3),
        (send_pair, 3), (add_pair, 0), (add_pair, 1), (encode, 4), (send_pair, 4), (add_pair, 2), (encode, 5),
        (send_pair, 5), (add_pair, 3), (add_pair, 4), (add_pair, 5), (add_ring, 0), (add_ring, 1), (add_ring, 2),
        (own, 0), (add_ring, 3), (own, 1), (add_ring, 4), (own, 2), (full, 0), (add_ring, 5), (own, 3), (full, 1),
        (own, 4), (full, 2), (onward, 0), (far, 0), (own, 5), (finish, 0), (full, 3), (onward, 1), (far, 1), (full, 4),
        (finish, 1), (onward, 2), (far, 2), (full, 5), (finish, 2), (onward, 3), (far, 3), (finish, 3), (onward, 4),
        (far, 4), (finish, 4), (onward, 5), (far, 5), (finish, 5),
    )
    for act, *which in plan:
        act(*which)

    for one in sent:
        one.wait_send()


STORES = 8


def store(base_v, mom_v, base_hbm, mom_hbm, sem):
    rows = base_v.shape[0] // STORES
    copies = [
        pltpu.make_async_copy(base_v.at[pl.ds(i * rows, rows)], base_hbm.at[pl.ds(i * rows, rows)], sem.at[i])
        for i in range(STORES)
    ]
    copies.append(pltpu.make_async_copy(mom_v, mom_hbm, sem.at[STORES]))
    for one in copies:
        one.start()
    for one in copies:
        one.wait()


def step(local_w, base_w, momentum):
    rows, columns = base_w.shape
    tiles = columns // (256 * PIECES)
    dma = pltpu.SemaphoreType.DMA
    chunk = (GROUP, tiles * BLOCK)
    ring = (PIECES, ZS) + chunk
    held = (CORES, PIECES, XS, ZS) + chunk
    each = dma((PIECES,))
    new_base, new_momentum = pl.pallas_call(
        functools.partial(kernel, tiles),
        out_shape=(pltpu.VMEM(base_w.shape, F32), pltpu.VMEM(momentum.shape, F32)),
        in_specs=[pl.BlockSpec(memory_space=pl.ANY)] * 3,
        out_specs=[pl.BlockSpec(memory_space=pltpu.VMEM)] * 2,
        scratch_shapes=[
            pltpu.VMEM((rows, columns), BF16),
            pltpu.VMEM((rows, columns), F32),
            pltpu.VMEM((ROWS, columns), F32),
            pltpu.VMEM((2 * BLOCK, 2 * BLOCK), BF16),
            pltpu.VMEM((2 * BLOCK, 2 * BLOCK), BF16),
            pltpu.VMEM(held, BF16),
            pltpu.VMEM((PIECES, XS, ZS) + chunk, BF16),
            pltpu.VMEM(ring, BF16),
            pltpu.VMEM(ring, BF16),
            pltpu.VMEM(ring, BF16),
            pltpu.VMEM((PIECES, ZS - 1) + chunk, BF16),
            pltpu.VMEM(ring, BF16),
            pltpu.VMEM((PIECES,) + chunk, F32),
            pltpu.VMEM(held, BF16),
            dma((PIECES, 2)), dma,
            each, each, each, each, each, each, each, each,
            dma((PIECES, ZS - 1)), dma((PIECES, ZS)),
            dma((PIECES, ZS - 1)), dma((PIECES, ZS)),
            dma((PIECES, 2)), dma((PIECES, 2)),
            each, each,
            dma((PIECES, 4)), dma((PIECES, 4)),
        ],
        compiler_params=pltpu.CompilerParams(
            collective_id=0, has_side_effects=True, vmem_limit_bytes=50 * 1024 * 1024
        ),
    )(*(pltpu.with_memory_space_constraint(a, pltpu.HBM) for a in (local_w, base_w, momentum)))
    return pl.pallas_call(
        store,
        out_shape=(jax.ShapeDtypeStruct(base_w.shape, F32), jax.ShapeDtypeStruct(momentum.shape, F32)),
        in_specs=[pl.BlockSpec(memory_space=pltpu.VMEM)] * 2,
        out_specs=[pl.BlockSpec(memory_space=pl.ANY)] * 2,
        scratch_shapes=[dma((STORES + 1,))],
        compiler_params=pltpu.CompilerParams(vmem_limit_bytes=4 * 1024 * 1024),
    )(*(pltpu.with_memory_space_constraint(a, pltpu.VMEM) for a in (new_base, new_momentum)))


def solution(mesh):
    in_specs = (P("worker", "shard", None), P("shard", None), P(("shard", "worker"), None))
    out_specs = (P("shard", None), P(("shard", "worker"), None))
    return jax.shard_map(step, mesh=mesh, in_specs=in_specs, out_specs=out_specs, check_vma=False)
```

```python
import functools
import math

import jax
import jax.numpy as jnp
from jax import lax
from jax.experimental import pallas as pl
from jax.experimental.pallas import tpu as pltpu
from jax.sharding import PartitionSpec as P

MESH = pl.DeviceIdType.MESH
F32 = jnp.float32
BF16 = jnp.bfloat16

BLOCK = 128
WORKERS = 32
EPSILON = 1e-06
CODE_LIMIT = 448.0
CLIP_WIDTH = 2.0
NESTEROV_MU = 0.9
OUTER_RATE = 0.7
ROOT = math.sqrt(BLOCK)

SIDE, CORES = 4, 2
ROWS = 8
GROUP = 16
STORES = 8
X, Z = 0, 1
PIECES = ((3, X, X), (3, Z, X), (3, X, X), (3, X, X), (3, X, Z), (3, X, X),)
COUNT = len(PIECES)


def signs(size):
    row = lax.broadcasted_iota(jnp.int32, (size, size), 0)
    col = lax.broadcasted_iota(jnp.int32, (size, size), 1)
    common = jnp.bitwise_and(jnp.bitwise_and(row, col), BLOCK - 1)
    for shift in (4, 2, 1):
        common = jnp.bitwise_xor(common, jnp.right_shift(common, shift))
    sign = (1 - 2 * jnp.bitwise_and(common, 1)).astype(F32)
    same = jnp.right_shift(row, 7) == jnp.right_shift(col, 7)
    return jnp.where(same, sign, 0.0).astype(BF16), jnp.where(same, 1.0, 0.0).astype(BF16)


def limit_of(square_sum):
    mean = square_sum * (1.0 / BLOCK) + EPSILON
    scale = (mean * lax.rsqrt(mean) * (CLIP_WIDTH / CODE_LIMIT)).astype(BF16)
    return scale.astype(F32)


def rotate_exactly(values, table):
    high = values.astype(BF16)
    low = (values - high.astype(F32)).astype(BF16)
    return jnp.dot(high, table, preferred_element_type=F32) + jnp.dot(low, table, preferred_element_type=F32)


def kernel(
    local_hbm, base_hbm, mom_hbm,
    out_v, out_mom,
    local_v, base_v, mom_v, table2, ones2,
    enc, sib, ring, part, parts, acc, gath,
    in_sem, mom_sem,
    sib_s, sib_r, ring_s, ring_r, part_s, part_r,
    near_s, near_r, own_s, own_r, rest_s, rest_r, pair_s, pair_r,
):
    me = lax.axis_index("worker")
    core = me % 2
    here = ((me // 2) % SIDE, me // 8)

    def at(x, z, c):
        return {"worker": (z * SIDE + x) * CORES + c}

    def peer(axis, off):
        there = list(here)
        there[axis] = (here[axis] + off) % SIDE
        return at(*there, core)

    pair = at(*here, 1 - core)
    offsets = (2, 1, 3)

    def copy(src, dst, send, recv, device):
        return pltpu.make_async_remote_copy(
            src_ref=src, dst_ref=dst, send_sem=send, recv_sem=recv, device_id=device, device_id_type=MESH
        )

    sent = []

    def start(*args):
        one = copy(*args)
        one.start()
        sent.append(one)

    def arrived(spot, send, recv):
        copy(spot, spot, send, recv, pair).wait_recv()

    firsts = [sum(size for size, _, _ in PIECES[:k]) for k in range(COUNT)]
    loads = []
    for k, (size, _, _) in enumerate(PIECES):
        cols = pl.ds(firsts[k] * 256, size * 256)
        loads.append((
            pltpu.make_async_copy(base_hbm.at[:, cols], base_v.at[:, cols], in_sem.at[k, 0]),
            pltpu.make_async_copy(local_hbm.at[0, :, cols], local_v.at[:, cols], in_sem.at[k, 1]),
        ))
        for one in loads[k]:
            one.start()
    mom_load = pltpu.make_async_copy(mom_hbm, mom_v, mom_sem)
    mom_load.start()

    barrier = pltpu.get_barrier_semaphore()
    greeted = [pair] + [peer(axis, off) for axis in (X, Z) for off in offsets]
    for device in greeted:
        pl.semaphore_signal(barrier, inc=1, device_id=device, device_id_type=MESH)

    table, ones = signs(2 * BLOCK)
    table2[...] = table
    ones2[...] = ones

    def enter():
        pl.semaphore_wait(barrier, len(greeted))

    def tile(t):
        return slice(t * BLOCK, (t + 1) * BLOCK)

    def stacked(size, read):
        return jnp.concatenate([read(t) for t in range(size)], axis=0)

    def cut(array, t):
        return array[t * GROUP : (t + 1) * GROUP]

    def encode(k):
        size, first_axis, _ = PIECES[k]
        for one in loads[k]:
            one.wait()
        for z in range(SIDE):
            rows = slice(z * SIDE * GROUP, (z + 1) * SIDE * GROUP)
            for t in range(size):
                cols = slice((firsts[k] + t) * 256, (firsts[k] + t + 1) * 256)
                diff = base_v[rows, cols] - local_v[rows, cols].astype(F32)
                turned = jnp.dot(diff.astype(BF16), table2[...], preferred_element_type=F32)
                square = jnp.dot((diff * diff).astype(BF16), ones2[...], preferred_element_type=F32)
                limit = limit_of(square) * (CODE_LIMIT * ROOT)
                value = jnp.minimum(jnp.maximum(turned, -limit), limit)
                for x in range(SIDE):
                    spot = (x, z) if first_axis == X else (z, x)
                    for c in range(CORES):
                        r = x * GROUP + c * ROWS
                        both = jnp.concatenate([value[r : r + ROWS, :BLOCK], value[r : r + ROWS, BLOCK:]], axis=0)
                        enc[k][c, *spot, :, tile(t)] = both.astype(BF16)

    def send_pair(k):
        start(enc[k].at[1 - core], sib[k], sib_s.at[k], sib_r.at[k], pair)

    def add_pair(k):
        axis = PIECES[k][1]
        arrived(sib[k], sib_s.at[k], sib_r.at[k])
        for off in offsets + (0,):
            to = (here[axis] + off) % SIDE
            enc[k][core, to] = (enc[k][core, to].astype(F32) + sib[k][to].astype(F32)).astype(BF16)
            if off:
                start(
                    enc[k].at[core, to], ring[k].at[off - 1], ring_s.at[k, off - 1], ring_r.at[k, off - 1],
                    peer(axis, off),
                )

    def add_first(k):
        axis = PIECES[k][1]
        for off in offsets:
            arrived(ring[k].at[off - 1], ring_s.at[k, off - 1], ring_r.at[k, off - 1])

        def total(to):
            there = enc[k][core, here[axis], to].astype(F32)
            for off in offsets:
                there = there + ring[k][off - 1, to].astype(F32)
            return there

        for off in offsets:
            part[k][off - 1] = total((here[1 - axis] + off) % SIDE).astype(BF16)
            start(
                part[k].at[off - 1], parts[k].at[off - 1], part_s.at[k, off - 1], part_r.at[k, off - 1],
                peer(1 - axis, off),
            )
        acc[k][...] = total(here[1 - axis])

    def own(k):
        if k == 0:
            mom_load.wait()
        size, _, axis = PIECES[k]
        table1 = table2[:BLOCK, :BLOCK]
        summed = acc[k][...]
        for off in offsets:
            arrived(parts[k].at[off - 1], part_s.at[k, off - 1], part_r.at[k, off - 1])
            summed = summed + parts[k][off - 1].astype(F32)
        total = stacked(size, lambda t: summed[:, tile(t)])
        blocks = [2 * (firsts[k] + t) for t in range(size)]
        momentum = stacked(
            size, lambda t: jnp.concatenate([mom_v[:, tile(blocks[t])], mom_v[:, tile(blocks[t] + 1)]], axis=0)
        )
        pseudo = rotate_exactly(total, table1) * (1.0 / (BLOCK * WORKERS))
        new_momentum = NESTEROV_MU * momentum + pseudo
        outer_step = pseudo + NESTEROV_MU * new_momentum
        square = jnp.sum(outer_step * outer_step, axis=-1, keepdims=True)
        limit = limit_of(square) * CODE_LIMIT
        turned = rotate_exactly(outer_step, table1) * (1.0 / ROOT)
        value = jnp.minimum(jnp.maximum(turned, -limit), limit).astype(BF16)
        for t in range(size):
            gath[k][core, here[axis], 0, :, tile(t)] = cut(value, t)
        spot = gath[k].at[core, here[axis], 0]
        for off in offsets:
            start(
                spot, gath[k].at[core, here[axis], SIDE - off], near_s.at[k, off - 1], near_r.at[k, off - 1],
                peer(1 - axis, off),
            )
        for off in offsets:
            start(spot, spot, own_s.at[k, off - 1], own_r.at[k, off - 1], peer(axis, off))
        for t in range(size):
            for b in range(2):
                out_mom[:, tile(blocks[t] + b)] = cut(new_momentum, t)[b * ROWS : (b + 1) * ROWS]

    def to_pair(k, i, place):
        spot = gath[k].at[core, place]
        start(spot, spot, pair_s.at[k, i], pair_r.at[k, i], pair)

    def spread(k):
        axis = PIECES[k][2]
        place = here[axis]
        for off in offsets:
            arrived(gath[k].at[core, place, SIDE - off], near_s.at[k, off - 1], near_r.at[k, off - 1])
        spot = gath[k].at[core, place, pl.ds(1, SIDE - 1)]
        for off in offsets:
            start(spot, spot, rest_s.at[k, off - 1], rest_r.at[k, off - 1], peer(axis, off))
        to_pair(k, 0, place)

    def collect(k):
        axis = PIECES[k][2]
        for off in (1, 3, 2):
            place = (here[axis] + SIDE - off) % SIDE
            arrived(gath[k].at[core, place, 0], own_s.at[k, off - 1], own_r.at[k, off - 1])
            arrived(gath[k].at[core, place, pl.ds(1, SIDE - 1)], rest_s.at[k, off - 1], rest_r.at[k, off - 1])
            to_pair(k, off, place)

    def decode(k, c, place):
        size, _, axis = PIECES[k]
        table1 = table2[:BLOCK, :BLOCK]
        codes = jnp.concatenate(
            [stacked(size, lambda t: gath[k][c, place, n, :, tile(t)]) for n in range(SIDE)], axis=0
        )
        back = jnp.dot(codes, table1, preferred_element_type=F32) * (OUTER_RATE / ROOT)
        for n in range(SIDE):
            near = (here[1 - axis] + n) % SIDE
            x, z = (place, near) if axis == X else (near, place)
            rows = pl.ds(pl.multiple_of((z * SIDE + x) * GROUP + c * ROWS, ROWS), ROWS)
            for t in range(size):
                for b in range(2):
                    cols = tile(2 * (firsts[k] + t) + b)
                    out_v[rows, cols] = base_v[rows, cols] - cut(back, n * size + t)[b * ROWS : (b + 1) * ROWS]

    def finish(k):
        axis = PIECES[k][2]
        places = [(here[axis] + SIDE - off) % SIDE for off in range(SIDE)]
        for off in (0, 1, 3, 2):
            decode(k, core, places[off])
        for off in (0, 1, 3, 2):
            arrived(gath[k].at[1 - core, places[off]], pair_s.at[k, off], pair_r.at[k, off])
            decode(k, 1 - core, places[off])

    plan = (
        (encode, 0), (enter,), (send_pair, 0), (encode, 1), (send_pair, 1), (encode, 2), (send_pair, 2), (encode, 3),
        (send_pair, 3), (add_pair, 0), (add_pair, 1), (encode, 4), (send_pair, 4), (add_pair, 2), (add_pair, 3),
        (encode, 5), (send_pair, 5), (add_pair, 4), (add_pair, 5), (add_first, 0), (add_first, 2), (add_first, 1),
        (add_first, 3), (own, 0), (add_first, 4), (own, 2), (add_first, 5), (own, 3), (own, 1), (spread, 0), (own, 4),
        (spread, 2), (own, 5), (collect, 0), (spread, 3), (spread, 4), (spread, 1), (finish, 0), (collect, 2),
        (finish, 2), (spread, 5), (collect, 3), (finish, 3), (collect, 1), (finish, 1), (collect, 4), (collect, 5),
        (finish, 4), (finish, 5),
    )
    for act, *which in plan:
        act(*which)

    for one in sent:
        one.wait_send()


def store(base_v, mom_v, base_hbm, mom_hbm, sem):
    rows = base_v.shape[0] // STORES
    copies = [
        pltpu.make_async_copy(base_v.at[pl.ds(i * rows, rows)], base_hbm.at[pl.ds(i * rows, rows)], sem.at[i])
        for i in range(STORES)
    ]
    copies.append(pltpu.make_async_copy(mom_v, mom_hbm, sem.at[STORES]))
    for one in copies:
        one.start()
    for one in copies:
        one.wait()


def step(local_w, base_w, momentum):
    rows, columns = base_w.shape
    dma = pltpu.SemaphoreType.DMA
    three = dma((COUNT, SIDE - 1))

    def each(*dims, dtype=BF16):
        return [pltpu.VMEM(dims + (GROUP, size * BLOCK), dtype) for size, _, _ in PIECES]

    new_base, new_momentum = pl.pallas_call(
        kernel,
        out_shape=(pltpu.VMEM(base_w.shape, F32), pltpu.VMEM(momentum.shape, F32)),
        in_specs=[pl.BlockSpec(memory_space=pl.ANY)] * 3,
        out_specs=[pl.BlockSpec(memory_space=pltpu.VMEM)] * 2,
        scratch_shapes=[
            pltpu.VMEM((rows, columns), BF16),
            pltpu.VMEM((rows, columns), F32),
            pltpu.VMEM((ROWS, columns), F32),
            pltpu.VMEM((2 * BLOCK, 2 * BLOCK), BF16),
            pltpu.VMEM((2 * BLOCK, 2 * BLOCK), BF16),
            each(CORES, SIDE, SIDE),
            each(SIDE, SIDE),
            each(SIDE - 1, SIDE),
            each(SIDE - 1),
            each(SIDE - 1),
            each(dtype=F32),
            each(CORES, SIDE, SIDE),
            dma((COUNT, 2)), dma,
            dma((COUNT,)), dma((COUNT,)), three, three, three, three,
            three, three, three, three, three, three, dma((COUNT, SIDE)), dma((COUNT, SIDE)),
        ],
        compiler_params=pltpu.CompilerParams(
            collective_id=0, has_side_effects=True, vmem_limit_bytes=50 * 1024 * 1024
        ),
    )(*(pltpu.with_memory_space_constraint(a, pltpu.HBM) for a in (local_w, base_w, momentum)))
    return pl.pallas_call(
        store,
        out_shape=(jax.ShapeDtypeStruct(base_w.shape, F32), jax.ShapeDtypeStruct(momentum.shape, F32)),
        in_specs=[pl.BlockSpec(memory_space=pltpu.VMEM)] * 2,
        out_specs=[pl.BlockSpec(memory_space=pl.ANY)] * 2,
        scratch_shapes=[dma((STORES + 1,))],
        compiler_params=pltpu.CompilerParams(vmem_limit_bytes=4 * 1024 * 1024),
    )(*(pltpu.with_memory_space_constraint(a, pltpu.VMEM) for a in (new_base, new_momentum)))


def solution(mesh):
    in_specs = (P("worker", "shard", None), P("shard", None), P(("shard", "worker"), None))
    out_specs = (P("shard", None), P(("shard", "worker"), None))
    return jax.shard_map(step, mesh=mesh, in_specs=in_specs, out_specs=out_specs, check_vma=False)
```

```python
import functools
import math

import jax
import jax.numpy as jnp
from jax import lax
from jax.experimental import pallas as pl
from jax.experimental.pallas import tpu as pltpu
from jax.sharding import PartitionSpec as P

MESH = pl.DeviceIdType.MESH
F32 = jnp.float32
BF16 = jnp.bfloat16

BLOCK = 128
WORKERS = 32
EPSILON = 1e-06
CODE_LIMIT = 448.0
CLIP_WIDTH = 2.0
NESTEROV_MU = 0.9
OUTER_RATE = 0.7
ROOT = math.sqrt(BLOCK)

SIDE, CORES = 4, 2
ROWS = 8
GROUP = 16
STORES = 8
X, Z = 0, 1
PIECES = ((2, X, X), (2, Z, X), (2, X, X), (2, X, X), (2, X, X), (2, X, X), (2, X, Z), (2, X, X), (2, X, X),)
COUNT = len(PIECES)
EARLY = (0, 1, 2, 3)


def signs(size):
    row = lax.broadcasted_iota(jnp.int32, (size, size), 0)
    col = lax.broadcasted_iota(jnp.int32, (size, size), 1)
    common = jnp.bitwise_and(jnp.bitwise_and(row, col), BLOCK - 1)
    for shift in (4, 2, 1):
        common = jnp.bitwise_xor(common, jnp.right_shift(common, shift))
    sign = (1 - 2 * jnp.bitwise_and(common, 1)).astype(F32)
    same = jnp.right_shift(row, 7) == jnp.right_shift(col, 7)
    return jnp.where(same, sign, 0.0).astype(BF16), jnp.where(same, 1.0, 0.0).astype(BF16)


def limit_of(square_sum):
    mean = square_sum * (1.0 / BLOCK) + EPSILON
    scale = (mean * lax.rsqrt(mean) * (CLIP_WIDTH / CODE_LIMIT)).astype(BF16)
    return scale.astype(F32)


def rotate_exactly(values, table):
    high = values.astype(BF16)
    low = (values - high.astype(F32)).astype(BF16)
    return jnp.dot(high, table, preferred_element_type=F32) + jnp.dot(low, table, preferred_element_type=F32)


def kernel(
    local_hbm, base_hbm, mom_hbm,
    out_v, out_mom,
    local_v, base_v, mom_v, table2, ones2,
    enc, sib, ring, part, parts, acc, gath,
    in_sem, mom_sem,
    sib_s, sib_r, ring_s, ring_r, part_s, part_r,
    near_s, near_r, far_s, far_r, pair_s, pair_r,
):
    me = lax.axis_index("worker")
    core = me % 2
    here = ((me // 2) % SIDE, me // 8)

    def at(x, z, c):
        return {"worker": (z * SIDE + x) * CORES + c}

    def peer(axis, off):
        there = list(here)
        there[axis] = (here[axis] + off) % SIDE
        return at(*there, core)

    pair = at(*here, 1 - core)
    offsets = (2, 1, 3)

    def copy(src, dst, send, recv, device):
        return pltpu.make_async_remote_copy(
            src_ref=src, dst_ref=dst, send_sem=send, recv_sem=recv, device_id=device, device_id_type=MESH
        )

    def start(*args):
        copy(*args).start()

    def arrived(spot, recv):
        copy(spot, spot, in_sem.at[0, 0], recv, pair).wait_recv()

    def left(spot, send):
        copy(spot, spot, send, in_sem.at[0, 0], pair).wait_send()

    firsts = [sum(size for size, _, _ in PIECES[:k]) for k in range(COUNT)]
    loads = []
    for k, (size, _, _) in enumerate(PIECES):
        cols = pl.ds(firsts[k] * 256, size * 256)
        loads.append((
            pltpu.make_async_copy(base_hbm.at[:, cols], base_v.at[:, cols], in_sem.at[k, 0]),
            pltpu.make_async_copy(local_hbm.at[0, :, cols], local_v.at[:, cols], in_sem.at[k, 1]),
        ))
        for one in loads[k]:
            one.start()
    mom_load = pltpu.make_async_copy(mom_hbm, mom_v, mom_sem)
    mom_load.start()

    barrier = pltpu.get_barrier_semaphore()
    greeted = [pair] + [peer(axis, off) for axis in (X, Z) for off in offsets]
    for device in greeted:
        pl.semaphore_signal(barrier, inc=1, device_id=device, device_id_type=MESH)

    table, ones = signs(2 * BLOCK)
    table2[...] = table
    ones2[...] = ones

    def enter():
        pl.semaphore_wait(barrier, len(greeted))

    def tile(t):
        return slice(t * BLOCK, (t + 1) * BLOCK)

    def stacked(size, read):
        return jnp.concatenate([read(t) for t in range(size)], axis=0)

    def cut(array, t):
        return array[t * GROUP : (t + 1) * GROUP]

    def encode(k):
        size, first_axis, _ = PIECES[k]
        for one in loads[k]:
            one.wait()
        for z in range(SIDE):
            rows = slice(z * SIDE * GROUP, (z + 1) * SIDE * GROUP)
            for t in range(size):
                cols = slice((firsts[k] + t) * 256, (firsts[k] + t + 1) * 256)
                diff = base_v[rows, cols] - local_v[rows, cols].astype(F32)
                turned = jnp.dot(diff.astype(BF16), table2[...], preferred_element_type=F32)
                square = jnp.dot((diff * diff).astype(BF16), ones2[...], preferred_element_type=F32)
                limit = limit_of(square) * (CODE_LIMIT * ROOT)
                value = jnp.minimum(jnp.maximum(turned, -limit), limit)
                for x in range(SIDE):
                    spot = (x, z) if first_axis == X else (z, x)
                    for c in range(CORES):
                        r = x * GROUP + c * ROWS
                        both = jnp.concatenate([value[r : r + ROWS, :BLOCK], value[r : r + ROWS, BLOCK:]], axis=0)
                        enc[k][c, *spot, :, tile(t)] = both.astype(BF16)

    def send_pair(k):
        start(enc[k].at[1 - core], sib[k], sib_s.at[k], sib_r.at[k], pair)

    def add_pair(k):
        axis = PIECES[k][1]
        arrived(sib[k], sib_r.at[k])
        for off in offsets + (0,):
            to = (here[axis] + off) % SIDE
            enc[k][core, to] = (enc[k][core, to].astype(F32) + sib[k][to].astype(F32)).astype(BF16)
            if off:
                start(enc[k].at[core, to], ring[k].at[off - 1], ring_s.at[k], ring_r.at[k], peer(axis, off))

    def add_first(k):
        axis = PIECES[k][1]
        arrived(ring[k], ring_r.at[k])

        def total(to):
            there = enc[k][core, here[axis], to].astype(F32)
            for off in offsets:
                there = there + ring[k][off - 1, to].astype(F32)
            return there

        for off in offsets:
            part[k][off - 1] = total((here[1 - axis] + off) % SIDE).astype(BF16)
            start(part[k].at[off - 1], parts[k].at[off - 1], part_s.at[k], part_r.at[k], peer(1 - axis, off))
        acc[k][...] = total(here[1 - axis])

    def own(k):
        if k == 0:
            mom_load.wait()
        size, _, axis = PIECES[k]
        table1 = table2[:BLOCK, :BLOCK]
        summed = acc[k][...]
        arrived(parts[k], part_r.at[k])
        for off in offsets:
            summed = summed + parts[k][off - 1].astype(F32)
        total = stacked(size, lambda t: summed[:, tile(t)])
        blocks = [2 * (firsts[k] + t) for t in range(size)]
        momentum = stacked(
            size, lambda t: jnp.concatenate([mom_v[:, tile(blocks[t])], mom_v[:, tile(blocks[t] + 1)]], axis=0)
        )
        pseudo = rotate_exactly(total, table1) * (1.0 / (BLOCK * WORKERS))
        new_momentum = NESTEROV_MU * momentum + pseudo
        outer_step = pseudo + NESTEROV_MU * new_momentum
        square = jnp.sum(outer_step * outer_step, axis=-1, keepdims=True)
        limit = limit_of(square) * CODE_LIMIT
        turned = rotate_exactly(outer_step, table1) * (1.0 / ROOT)
        value = jnp.minimum(jnp.maximum(turned, -limit), limit).astype(BF16)
        for t in range(size):
            gath[k][core, here[axis], 0, :, tile(t)] = cut(value, t)
        spot = gath[k].at[core, here[axis], 0]
        for off in offsets:
            start(spot, gath[k].at[core, here[axis], SIDE - off], near_s.at[k], near_r.at[k], peer(1 - axis, off))
        if k in EARLY:
            for off in offsets:
                start(spot, spot, far_s.at[k], far_r.at[k, off - 1], peer(axis, off))
        for t in range(size):
            for b in range(2):
                out_mom[:, tile(blocks[t] + b)] = cut(new_momentum, t)[b * ROWS : (b + 1) * ROWS]

    def to_pair(k, place):
        spot = gath[k].at[core, place]
        start(spot, spot, pair_s.at[k], pair_r.at[k], pair)

    def spread(k):
        axis = PIECES[k][2]
        place = here[axis]
        spot = gath[k].at[core, place, pl.ds(1, SIDE - 1)]
        arrived(spot, near_r.at[k])
        if k not in EARLY:
            spot = gath[k].at[core, place]
        for off in offsets:
            start(spot, spot, far_s.at[k], far_r.at[k, off - 1], peer(axis, off))
        to_pair(k, place)
        left(sib[k], sib_s.at[k])
        left(ring[k], ring_s.at[k])
        left(part[k], part_s.at[k])

    def collect(k):
        axis = PIECES[k][2]
        for off in (1, 3, 2):
            place = (here[axis] + SIDE - off) % SIDE
            arrived(gath[k].at[core, place], far_r.at[k, off - 1])
            to_pair(k, place)

    def decode(k, c, place):
        size, _, axis = PIECES[k]
        table1 = table2[:BLOCK, :BLOCK]
        codes = jnp.concatenate(
            [stacked(size, lambda t: gath[k][c, place, n, :, tile(t)]) for n in range(SIDE)], axis=0
        )
        back = jnp.dot(codes, table1, preferred_element_type=F32) * (OUTER_RATE / ROOT)
        for n in range(SIDE):
            near = (here[1 - axis] + n) % SIDE
            x, z = (place, near) if axis == X else (near, place)
            rows = pl.ds(pl.multiple_of((z * SIDE + x) * GROUP + c * ROWS, ROWS), ROWS)
            for t in range(size):
                for b in range(2):
                    cols = tile(2 * (firsts[k] + t) + b)
                    out_v[rows, cols] = base_v[rows, cols] - cut(back, n * size + t)[b * ROWS : (b + 1) * ROWS]

    def finish(k):
        axis = PIECES[k][2]
        places = [(here[axis] + SIDE - off) % SIDE for off in range(SIDE)]
        for off in (0, 1, 3, 2):
            decode(k, core, places[off])
        arrived(gath[k].at[1 - core], pair_r.at[k])
        for off in (0, 1, 3, 2):
            decode(k, 1 - core, places[off])
        left(part[k], near_s.at[k])
        left(ring[k], far_s.at[k])
        left(gath[k].at[core], pair_s.at[k])

    plan = (
        (encode, 0), (encode, 1), (enter,), (send_pair, 0), (send_pair, 1), (encode, 2), (send_pair, 2), (encode, 3),
        (send_pair, 3), (encode, 4), (send_pair, 4), (add_pair, 0), (add_pair, 1), (add_pair, 2), (encode, 5),
        (send_pair, 5), (add_pair, 3), (add_pair, 4), (encode, 6), (send_pair, 6), (encode, 7), (send_pair, 7),
        (add_pair, 5), (encode, 8), (send_pair, 8), (add_pair, 6), (add_pair, 7), (add_pair, 8), (add_first, 0),
        (add_first, 2), (add_first, 1), (add_first, 3), (own, 0), (add_first, 4), (own, 2), (add_first, 5), (own, 3),
        (add_first, 6), (spread, 0), (add_first, 7), (own, 4), (spread, 2), (add_first, 8), (own, 5), (own, 1),
        (spread, 3), (own, 6), (collect, 0), (own, 7), (spread, 4), (finish, 0), (collect, 2), (own, 8), (spread, 5),
        (finish, 2), (spread, 1), (collect, 3), (spread, 6), (spread, 7), (finish, 3), (collect, 4), (spread, 8),
        (finish, 4), (collect, 5), (collect, 1), (finish, 5), (collect, 7), (finish, 1), (collect, 6), (collect, 8),
        (finish, 7), (finish, 6), (finish, 8),
    )
    for act, *which in plan:
        act(*which)


def store(base_v, mom_v, base_hbm, mom_hbm, sem):
    rows = base_v.shape[0] // STORES
    copies = [
        pltpu.make_async_copy(base_v.at[pl.ds(i * rows, rows)], base_hbm.at[pl.ds(i * rows, rows)], sem.at[i])
        for i in range(STORES)
    ]
    copies.append(pltpu.make_async_copy(mom_v, mom_hbm, sem.at[STORES]))
    for one in copies:
        one.start()
    for one in copies:
        one.wait()


def step(local_w, base_w, momentum):
    rows, columns = base_w.shape
    dma = pltpu.SemaphoreType.DMA
    one = dma((COUNT,))

    def each(*dims, dtype=BF16):
        return [pltpu.VMEM(dims + (GROUP, size * BLOCK), dtype) for size, _, _ in PIECES]

    new_base, new_momentum = pl.pallas_call(
        kernel,
        out_shape=(pltpu.VMEM(base_w.shape, F32), pltpu.VMEM(momentum.shape, F32)),
        in_specs=[pl.BlockSpec(memory_space=pl.ANY)] * 3,
        out_specs=[pl.BlockSpec(memory_space=pltpu.VMEM)] * 2,
        scratch_shapes=[
            pltpu.VMEM((rows, columns), BF16),
            pltpu.VMEM((rows, columns), F32),
            pltpu.VMEM((ROWS, columns), F32),
            pltpu.VMEM((2 * BLOCK, 2 * BLOCK), BF16),
            pltpu.VMEM((2 * BLOCK, 2 * BLOCK), BF16),
            each(CORES, SIDE, SIDE),
            each(SIDE, SIDE),
            each(SIDE - 1, SIDE),
            each(SIDE - 1),
            each(SIDE - 1),
            each(dtype=F32),
            each(CORES, SIDE, SIDE),
            dma((COUNT, 2)), dma,
            one, one, one, one, one, one,
            one, one, one, dma((COUNT, SIDE - 1)), one, one,
        ],
        compiler_params=pltpu.CompilerParams(
            collective_id=0, has_side_effects=True, vmem_limit_bytes=50 * 1024 * 1024
        ),
    )(*(pltpu.with_memory_space_constraint(a, pltpu.HBM) for a in (local_w, base_w, momentum)))
    return pl.pallas_call(
        store,
        out_shape=(jax.ShapeDtypeStruct(base_w.shape, F32), jax.ShapeDtypeStruct(momentum.shape, F32)),
        in_specs=[pl.BlockSpec(memory_space=pltpu.VMEM)] * 2,
        out_specs=[pl.BlockSpec(memory_space=pl.ANY)] * 2,
        scratch_shapes=[dma((STORES + 1,))],
        compiler_params=pltpu.CompilerParams(vmem_limit_bytes=4 * 1024 * 1024),
    )(*(pltpu.with_memory_space_constraint(a, pltpu.VMEM) for a in (new_base, new_momentum)))


def solution(mesh):
    in_specs = (P("worker", "shard", None), P("shard", None), P(("shard", "worker"), None))
    out_specs = (P("shard", None), P(("shard", "worker"), None))
    return jax.shard_map(step, mesh=mesh, in_specs=in_specs, out_specs=out_specs, check_vma=False)
```
